512 devices in a mesh: dp: 16 (over y_lo, x, core), mp: 32 (over y_hi, z).
Axes of the slice: x: 4, y: 8 (y_hi: 4, y_lo: 2; y = y_hi * 2 + y_lo), z: 8, core: 2. Of those that a mesh axis runs over, the one named last changes fastest.
Arguments:
- activations: bfloat16 [8192, 6144], P('dp', 'mp'), may hold values from -400 to 400
- ln_gain: bfloat16 [6144], P('mp'), may hold values from 0.099609375 to 1.8984375
- task_ids: int32 [32], P('dp'), may hold values from 0 to 7
- w_qkv: bfloat16 [6144, 32, 384], P(None, 'mp'), may hold values from -0.078125 to 0.078125
- a_shared: bfloat16 [256, 6144], P('dp', 'mp'), may hold values from -0.078125 to 0.078125
- b_shared: bfloat16 [32, 128, 256], P('mp'), may hold values from -0.375 to 0.375
- d_query: float32 [8, 256], replicated, may hold values from -4 to 4
- d_value: float32 [8, 256], replicated, may hold values from -4 to 4
- b_query: float32 [8, 32, 128], P(None, 'mp'), may hold values from -4 to 4
- b_value: float32 [8, 32, 128], P(None, 'mp'), may hold values from -4 to 4
Outputs:
- attended: bfloat16 [8192, 32, 128], P('dp', 'mp')
The draws below stay inside these ranges and needn't reach their ends.
All inputs are finite; a program needn't handle non-finite values.
Results may differ from the reference program's by a relative error of at most 0.0087.
Values may be sent and summed in bfloat16 or wider, within the bound.
No kernel may reach another device: no remote copies, remote signals or barrier semaphores. Data moves between devices by JAX's collectives and lax.ppermute only.
A program may use at most 64 MiB of HBM per device.

```python
import jax
import jax.numpy as jnp
from jax import lax

D = 6144
HEADS = 32
HD = 128
R = 256
TASKS = 8
PATCH = 256
IMG_DP = 2
IMAGES = 32
TOKENS = 8192
TOK_GRP = 512
N_DP = 16


def draw_activations(key, part):
    key = jax.random.fold_in(key, 11)
    first, second, third = jax.random.split(key, 3)
    col_scale = jnp.exp(jax.random.uniform(third, (1, D), jnp.float32) * jnp.log(10.0))
    row_scale = jnp.exp(jax.random.uniform(second, (TOKENS, 1), jnp.float32) * jnp.log(10.0))
    base = jax.random.truncated_normal(first, -4.0, 4.0, (TOKENS, D), jnp.float32)
    return (base * row_scale * col_scale).astype(jnp.bfloat16)


def set_ends(values, rng, low, high):
    dims = values.shape
    index_at = [jax.random.randint(jax.random.fold_in(rng, axis), (), 0, dims[axis]) for axis in range(len(dims))]
    values = values.at[tuple(index_at)].set(low)
    longest = dims.index(max(dims))
    index_at[longest] = (index_at[longest] + 1) % dims[longest]
    return values.at[tuple(index_at)].set(high)


def block_levels(own_key, dims, cuts, smallest, top_value):
    loudness = 1.0
    for dim, parts in cuts:
        heights = jax.random.uniform(jax.random.fold_in(jax.random.fold_in(own_key, 6), dim), (parts,), jnp.float32, smallest / len(cuts), top_value / len(cuts))
        loudness = loudness * jnp.repeat(jnp.exp(heights), dims[dim] // parts).reshape((-1,) + (1,) * (len(dims) - 1 - dim))
    return loudness


def bell_draw(stream_key, shape, width, most, cuts=(), kind=jnp.bfloat16):
    values = width * jax.random.normal(stream_key, shape, jnp.float32)
    if cuts:
        values = values * block_levels(stream_key, shape, cuts, -0.22, 0.18)
    return jnp.clip(values, -most, most).astype(kind)


def setup_inputs(seed: int = 0) -> dict:
    key_of = jax.random.split(jax.random.key(seed), 11)
    activations = draw_activations(jax.random.fold_in(key_of[10], 71), 0)
    ln_gain = jnp.clip(1.0 + 0.18 * jax.random.normal(key_of[1], (D,), jnp.float32), 0.099609375, 1.8984375).astype(jnp.bfloat16)
    task_ids = set_ends(jax.random.randint(key_of[2], (IMAGES,), 0, TASKS), jax.random.fold_in(key_of[2], 1), 0, TASKS - 1).astype(jnp.int32)
    w_qkv = bell_draw(key_of[3], (D, HEADS, 3 * HD), D ** -0.5, 0.078125, ((1, 32),))
    a_shared = bell_draw(key_of[4], (R, D), D ** -0.5, 0.078125, ((0, 16), (1, 32)))
    b_shared = bell_draw(key_of[5], (HEADS, HD, R), R ** -0.5, 0.375, ((0, 32),))
    d_query = bell_draw(key_of[6], (TASKS, R), 1.0, 4.0, (), jnp.float32)
    d_value = bell_draw(key_of[7], (TASKS, R), 1.0, 4.0, (), jnp.float32)
    b_query = bell_draw(key_of[8], (TASKS, HEADS, HD), 0.7, 4.0, ((1, 32),), jnp.float32)
    b_value = bell_draw(key_of[9], (TASKS, HEADS, HD), 1.0, 4.0, ((1, 32),), jnp.float32)
    return {"activations": activations, "ln_gain": ln_gain, "task_ids": task_ids, "w_qkv": w_qkv, "a_shared": a_shared, "b_shared": b_shared, "d_query": d_query, "d_value": d_value, "b_query": b_query, "b_value": b_value}


def unit_rows(values):
    centre = values - lax.optimization_barrier(jnp.mean(values, axis=-1, keepdims=True))
    spread = lax.optimization_barrier(jnp.mean(centre * centre, axis=-1, keepdims=True))
    return centre * lax.rsqrt(spread + 1e-06)

def reference(activations, ln_gain, task_ids, w_qkv, a_shared, b_shared, d_query, d_value, b_query, b_value):

    def one_group(carry, inputs):
        group_rows, tasks = inputs
        normed = (unit_rows(group_rows.astype(jnp.float32)) * ln_gain.astype(jnp.float32)).astype(jnp.bfloat16)
        qkv = jnp.dot(normed, w_qkv.reshape(D, HEADS * 3 * HD), preferred_element_type=jnp.float32)
        qkv = qkv.reshape(IMG_DP, PATCH, HEADS, 3, HD)
        ranks = jnp.dot(normed, a_shared.T, preferred_element_type=jnp.float32).reshape(IMG_DP, PATCH, R)
        scaled_q = (ranks * jnp.take(d_query, tasks, axis=0)[:, None, :]).astype(jnp.bfloat16)
        scaled_v = (ranks * jnp.take(d_value, tasks, axis=0)[:, None, :]).astype(jnp.bfloat16)
        b_mat = b_shared.reshape(HEADS * HD, R).T
        up_q = jnp.dot(scaled_q.reshape(TOK_GRP, R), b_mat, preferred_element_type=jnp.float32)
        up_v = jnp.dot(scaled_v.reshape(TOK_GRP, R), b_mat, preferred_element_type=jnp.float32)
        up_q = up_q.reshape(IMG_DP, PATCH, HEADS, HD)
        up_v = up_v.reshape(IMG_DP, PATCH, HEADS, HD)
        query = qkv[:, :, :, 0, :] + up_q * jnp.take(b_query, tasks, axis=0)[:, None]
        value = qkv[:, :, :, 2, :] + up_v * jnp.take(b_value, tasks, axis=0)[:, None]
        qn = unit_rows(query).astype(jnp.bfloat16)
        kn = unit_rows(qkv[:, :, :, 1, :]).astype(jnp.bfloat16)
        vb = value.astype(jnp.bfloat16)
        scores = jnp.einsum('iphd,iqhd->ihpq', qn.astype(jnp.float32), kn.astype(jnp.float32)) * (1.0 / jnp.sqrt(jnp.float32(HD)))
        expo = jnp.exp(scores)
        probs = (expo / lax.optimization_barrier(jnp.sum(expo, axis=-1, keepdims=True))).astype(jnp.bfloat16)
        result = jnp.einsum('ihpq,iqhd->iphd', probs.astype(jnp.float32), vb.astype(jnp.float32))
        return (carry, result.astype(jnp.bfloat16).reshape(TOK_GRP, HEADS, HD))
    grouped_rows = activations.reshape(N_DP, TOK_GRP, D)
    grouped_tasks = task_ids.reshape(N_DP, IMG_DP).astype(jnp.int32)
    unused, outputs = lax.scan(one_group, jnp.float32(0.0), (grouped_rows, grouped_tasks))
    return outputs.reshape(TOKENS, HEADS, HD)
```

```python
import jax
import jax.numpy as jnp
from jax import lax
from jax.experimental import pallas as pl
from jax.experimental.pallas import tpu as pltpu
from jax.sharding import PartitionSpec as P

eps = 1e-06
N_Y, N_Z = 4, 8
along_y = [[y * N_Z + z for y in range(N_Y)] for z in range(N_Z)]
along_z = [[y * N_Z + z for z in range(N_Z)] for y in range(N_Y)]


def unit_columns(values):
    centre = values - jnp.mean(values, axis=0, keepdims=True)
    spread = jnp.mean(centre * centre, axis=0, keepdims=True)
    return (centre * lax.rsqrt(spread + eps)).astype(jnp.bfloat16)


def heads_kernel(x_ref, w_ref, gain_ref, stat_ref, low_ref, b_ref, scale_ref, out_ref, acc_ref):
    step = pl.program_id(0)

    @pl.when(step == 0)
    def _():
        acc_ref[...] = jnp.zeros_like(acc_ref)

    gain = jnp.transpose(gain_ref[0])[:, :1]
    centre = x_ref[...].astype(jnp.float32) - stat_ref[0:1, :]
    normed = (centre * stat_ref[1:2, :] * gain).astype(jnp.bfloat16)
    acc_ref[...] += jnp.dot(w_ref[0], normed, preferred_element_type=jnp.float32)

    @pl.when(step == pl.num_programs(0) - 1)
    def _():
        size = b_ref.shape[0]
        images = scale_ref.shape[1] // 2
        patches = x_ref.shape[1] // images
        rank = b_ref.shape[1]
        up_q = jnp.dot(b_ref[...], low_ref[:rank], preferred_element_type=jnp.float32)
        up_v = jnp.dot(b_ref[...], low_ref[rank:], preferred_element_type=jnp.float32)
        for i in range(images):
            cols = slice(i * patches, (i + 1) * patches)
            query = acc_ref[:size, cols] + up_q[:, cols] * scale_ref[:, i : i + 1]
            value = (
                acc_ref[2 * size :, cols] + up_v[:, cols] * scale_ref[:, images + i : images + i + 1]
            ).astype(jnp.bfloat16)
            query = unit_columns(query)
            key = unit_columns(acc_ref[size : 2 * size, cols])
            scores = lax.dot_general(
                key, query, (((0,), (0,)), ((), ())), preferred_element_type=jnp.float32
            )
            expo = jnp.exp(scores * (1.0 / jnp.sqrt(jnp.float32(size))))
            probs = (expo / jnp.sum(expo, axis=0, keepdims=True)).astype(jnp.bfloat16)
            mixed = jnp.dot(value, probs, preferred_element_type=jnp.float32)
            out_ref[cols, :] = jnp.transpose(mixed).astype(out_ref.dtype)


def local(
    activations, ln_gain, task_ids, w_qkv, a_shared, b_shared, d_query, d_value, b_query, b_value
):
    rows, width = activations.shape
    images = task_ids.shape[0]
    patches = rows // images
    size = b_shared.shape[1]
    rank = b_shared.shape[2]
    tasks = d_query.shape[0]
    parts = lax.axis_size("mp")
    full = width * parts
    own = rank // parts

    flat = activations.T
    by_y = lax.all_gather(flat, "mp", axis=0, tiled=True, axis_index_groups=along_y)
    whole = lax.all_gather(by_y, "mp", axis=0, tiled=True, axis_index_groups=along_z)

    gain = ln_gain.astype(jnp.float32)
    down = lax.all_gather(a_shared, "dp", axis=0, tiled=True)
    values = flat.astype(jnp.float32)
    mean_here = jnp.mean(values, axis=0)
    centre = values - mean_here
    square_here = jnp.sum(centre * centre, axis=0)
    partial = jnp.dot(
        down, (centre * gain[:, None]).astype(jnp.bfloat16), preferred_element_type=jnp.float32
    )
    down_gain = jnp.sum(down.astype(jnp.float32) * gain, axis=1)
    extra = jnp.concatenate(
        (
            jnp.broadcast_to(mean_here, (parts, 1, rows)),
            jnp.broadcast_to(square_here, (parts, 1, rows)),
            jnp.concatenate(
                (
                    jnp.broadcast_to(gain, (parts, 1, width)),
                    down_gain.reshape(parts, 1, own),
                    jnp.zeros((parts, 1, rows - width - own), jnp.float32),
                ),
                axis=2,
            ),
        ),
        axis=1,
    )
    sent = jnp.concatenate((partial.reshape(parts, own, rows), extra), axis=1)
    came = lax.all_to_all(sent, "mp", 0, 0)
    means = came[:, own]
    row_mean = jnp.mean(means, axis=0)
    offset = means - row_mean
    row_var = (jnp.sum(came[:, own + 1], axis=0) + width * jnp.sum(offset * offset, axis=0)) / full
    row_scale = lax.rsqrt(row_var + eps)
    gains = came[:, own + 2, :width]
    ranks = jnp.sum(
        came[:, :own] + came[:, own + 2, width : width + own, None] * offset[:, None, :], axis=0
    )
    ranks = ranks * row_scale

    onehot = (task_ids[:, None] == lax.broadcasted_iota(jnp.int32, (images, tasks), 1)).astype(
        jnp.float32
    )
    highest = lax.Precision.HIGHEST
    at = lax.axis_index("mp") * own
    dq = jnp.dot(onehot, lax.dynamic_slice_in_dim(d_query, at, own, 1), precision=highest)
    dv = jnp.dot(onehot, lax.dynamic_slice_in_dim(d_value, at, own, 1), precision=highest)
    by_image = ranks.reshape(own, images, patches)
    scaled = jnp.stack((by_image * dq.T[:, :, None], by_image * dv.T[:, :, None]), axis=0)
    scaled = scaled.reshape(1, 2 * own, rows).astype(jnp.bfloat16)
    low = lax.all_to_all(jnp.broadcast_to(scaled, (parts, 2 * own, rows)), "mp", 0, 0)
    low = low.reshape(parts, 2, own, rows).transpose(1, 0, 2, 3).reshape(2 * rank, rows)

    bq = jnp.dot(onehot, b_query.reshape(tasks, size), precision=highest)
    bv = jnp.dot(onehot, b_value.reshape(tasks, size), precision=highest)
    scale = jnp.concatenate((bq, bv), axis=0).T
    stat = jnp.stack((row_mean, row_scale), axis=0)
    block = N_Y * width
    outs = w_qkv.shape[2]
    weights = (
        w_qkv.reshape(N_Y, N_Z, width, outs).transpose(1, 3, 0, 2).reshape(N_Z, outs, block)
    )
    gains = gains.reshape(N_Y, N_Z, width).transpose(1, 0, 2).reshape(N_Z, 1, block)
    gains = jnp.broadcast_to(gains, (N_Z, 8, block))

    result = pl.pallas_call(
        heads_kernel,
        grid=(N_Z,),
        in_specs=[
            pl.BlockSpec((block, rows), lambda i: (i, 0)),
            pl.BlockSpec((1, outs, block), lambda i: (i, 0, 0)),
            pl.BlockSpec((1, 8, block), lambda i: (i, 0, 0)),
            pl.BlockSpec((2, rows), lambda i: (0, 0)),
            pl.BlockSpec((2 * rank, rows), lambda i: (0, 0)),
            pl.BlockSpec((size, rank), lambda i: (0, 0)),
            pl.BlockSpec((size, 2 * images), lambda i: (0, 0)),
        ],
        out_specs=pl.BlockSpec((rows, size), lambda i: (0, 0)),
        out_shape=jax.ShapeDtypeStruct((rows, size), jnp.bfloat16),
        scratch_shapes=[pltpu.VMEM((outs, rows), jnp.float32)],
        compiler_params=pltpu.CompilerParams(
            dimension_semantics=("arbitrary",), vmem_limit_bytes=40 * 2**20
        ),
        cost_estimate=pl.CostEstimate(
            flops=2 * full * outs * rows, bytes_accessed=12 * 2**20, transcendentals=0
        ),
        name="heads",
    )(whole, weights, gains, stat, low, b_shared.reshape(size, rank), scale)
    return result.reshape(rows, 1, size)


def solution(mesh):
    return jax.shard_map(
        local,
        mesh=mesh,
        in_specs=(
            P("dp", "mp"),
            P("mp"),
            P("dp"),
            P(None, "mp", None),
            P("dp", "mp"),
            P("mp", None, None),
            P(),
            P(),
            P(None, "mp", None),
            P(None, "mp", None),
        ),
        out_specs=P("dp", "mp", None),
        check_vma=False,
    )
```

```python
import jax
import jax.numpy as jnp
from jax import lax
from jax.experimental import pallas as pl
from jax.experimental.pallas import tpu as pltpu
from jax.sharding import PartitionSpec as P

eps = 1e-06
N_Y, N_Z = 4, 8
along_y = [[y * N_Z + z for y in range(N_Y)] for z in range(N_Z)]
along_z = [[y * N_Z + z for z in range(N_Z)] for y in range(N_Y)]


def terms(values):
    high = lax.reduce_precision(values, 8, 7)
    rest = values - high
    middle = lax.reduce_precision(rest, 8, 7)
    return [part.astype(jnp.bfloat16) for part in (high, middle, rest - middle)]


def unit_columns(values):
    centre = values - jnp.mean(values, axis=0, keepdims=True)
    spread = jnp.mean(centre * centre, axis=0, keepdims=True)
    return (centre * lax.rsqrt(spread + eps)).astype(jnp.bfloat16)


def heads_kernel(x_ref, w_ref, gain_ref, stat_ref, low_ref, b_ref, scale_ref, out_ref, acc_ref):
    step = pl.program_id(0)

    @pl.when(step == 0)
    def _():
        acc_ref[...] = jnp.zeros_like(acc_ref)

    gain = jnp.transpose(gain_ref[0])[:, :1]
    centre = x_ref[...].astype(jnp.float32) - stat_ref[0:1, :]
    normed = (centre * stat_ref[1:2, :] * gain).astype(jnp.bfloat16)
    acc_ref[...] += jnp.dot(w_ref[0], normed, preferred_element_type=jnp.float32)

    @pl.when(step == pl.num_programs(0) - 1)
    def _():
        size = b_ref.shape[0]
        images = scale_ref.shape[1] // 2
        patches = x_ref.shape[1] // images
        rank = b_ref.shape[1]
        up_q = jnp.dot(b_ref[...], low_ref[:rank], preferred_element_type=jnp.float32)
        up_v = jnp.dot(b_ref[...], low_ref[rank:], preferred_element_type=jnp.float32)
        for i in range(images):
            cols = slice(i * patches, (i + 1) * patches)
            query = acc_ref[:size, cols] + up_q[:, cols] * scale_ref[:, i : i + 1]
            value = (
                acc_ref[2 * size :, cols] + up_v[:, cols] * scale_ref[:, images + i : images + i + 1]
            ).astype(jnp.bfloat16)
            query = unit_columns(query)
            key = unit_columns(acc_ref[size : 2 * size, cols])
            scores = lax.dot_general(
                key, query, (((0,), (0,)), ((), ())), preferred_element_type=jnp.float32
            )
            expo = jnp.exp(scores * (1.0 / jnp.sqrt(jnp.float32(size))))
            probs = (expo / jnp.sum(expo, axis=0, keepdims=True)).astype(jnp.bfloat16)
            mixed = jnp.dot(value, probs, preferred_element_type=jnp.float32)
            out_ref[cols, :] = jnp.transpose(mixed).astype(out_ref.dtype)


def local(
    activations, ln_gain, task_ids, w_qkv, a_shared, b_shared, d_query, d_value, b_query, b_value
):
    rows, width = activations.shape
    images = task_ids.shape[0]
    patches = rows // images
    size = b_shared.shape[1]
    rank = b_shared.shape[2]
    tasks = d_query.shape[0]
    parts = lax.axis_size("mp")
    full = width * parts
    own = rank // parts
    groups = lax.axis_size("dp")

    flat = activations.T
    by_y = lax.all_gather(flat, "mp", axis=0, tiled=True, axis_index_groups=along_y)
    whole = lax.all_gather(by_y, "mp", axis=0, tiled=True, axis_index_groups=along_z)

    block = N_Y * width
    quarter = rank // N_Y
    down = lax.all_to_all(jnp.broadcast_to(a_shared, (groups, rank // groups, width)), "dp", 0, 0)
    down = jnp.concatenate(
        (
            down.reshape(N_Y, quarter, width),
            jnp.broadcast_to(ln_gain, (N_Y, 1, width)),
            jnp.zeros((N_Y, 15, width), jnp.bfloat16),
        ),
        axis=1,
    )
    down = lax.all_to_all(down, "mp", 0, 0, axis_index_groups=along_y)
    gain = down[:, quarter].reshape(block)
    down = down[:, :quarter].transpose(1, 0, 2).reshape(quarter, block)
    values = by_y.astype(jnp.float32)
    mean_here = jnp.mean(values, axis=0)
    centre = values - mean_here
    square_here = jnp.sum(centre * centre, axis=0)
    gain_here = gain.astype(jnp.float32)
    partial = jnp.dot(
        down, (centre * gain_here[:, None]).astype(jnp.bfloat16), preferred_element_type=jnp.float32
    )
    down_gain = jnp.sum(down.astype(jnp.float32) * gain_here, axis=1).reshape(N_Z, own)
    lead = rows - (block - rows)
    last = jnp.concatenate(
        (
            *terms(down_gain),
            jnp.zeros((N_Z, lead - 3 * own), jnp.bfloat16),
            jnp.broadcast_to(gain, (N_Z, block)),
        ),
        axis=1,
    )
    stats = jnp.stack(terms(mean_here) + terms(square_here), axis=0)
    sent = jnp.concatenate(
        (
            partial.astype(jnp.bfloat16).reshape(N_Z, own, rows),
            jnp.broadcast_to(stats, (N_Z, 6, rows)),
            last.reshape(N_Z, 2, rows),
        ),
        axis=1,
    )
    came = lax.all_to_all(sent, "mp", 0, 0, axis_index_groups=along_z).astype(jnp.float32)
    means = came[:, own] + came[:, own + 1] + came[:, own + 2]
    squares = came[:, own + 3] + came[:, own + 4] + came[:, own + 5]
    side = came[:, own + 6 :].reshape(N_Z, 2 * rows)
    gains = side[:, lead:]
    down_gains = side[:, :own] + side[:, own : 2 * own] + side[:, 2 * own : 3 * own]
    row_mean = jnp.mean(means, axis=0)
    offset = means - row_mean
    row_var = (jnp.sum(squares, axis=0) + block * jnp.sum(offset * offset, axis=0)) / full
    row_scale = lax.rsqrt(row_var + eps)
    ranks = jnp.sum(came[:, :own] + down_gains[:, :, None] * offset[:, None, :], axis=0) * row_scale

    onehot = (task_ids[:, None] == lax.broadcasted_iota(jnp.int32, (images, tasks), 1)).astype(
        jnp.float32
    )
    highest = lax.Precision.HIGHEST
    at = lax.axis_index("mp") * own
    dq = jnp.dot(onehot, lax.dynamic_slice_in_dim(d_query, at, own, 1), precision=highest)
    dv = jnp.dot(onehot, lax.dynamic_slice_in_dim(d_value, at, own, 1), precision=highest)
    by_image = ranks.reshape(own, images, patches)
    scaled = jnp.stack((by_image * dq.T[:, :, None], by_image * dv.T[:, :, None]), axis=0)
    scaled = scaled.reshape(2 * own, rows).astype(jnp.bfloat16)
    low = lax.all_to_all(
        jnp.broadcast_to(scaled, (N_Z, 2 * own, rows)), "mp", 0, 0, axis_index_groups=along_z
    )
    low = lax.all_to_all(
        jnp.broadcast_to(low, (N_Y, N_Z, 2 * own, rows)), "mp", 0, 0, axis_index_groups=along_y
    )
    low = low.reshape(parts, 2, own, rows).transpose(1, 0, 2, 3).reshape(2 * rank, rows)

    bq = jnp.dot(onehot, b_query.reshape(tasks, size), precision=highest)
    bv = jnp.dot(onehot, b_value.reshape(tasks, size), precision=highest)
    scale = jnp.concatenate((bq, bv), axis=0).T
    stat = jnp.stack((row_mean, row_scale), axis=0)
    outs = w_qkv.shape[2]
    weights = (
        w_qkv.reshape(N_Y, N_Z, width, outs).transpose(1, 3, 0, 2).reshape(N_Z, outs, block)
    )
    gains = gains.reshape(N_Z, 1, block)
    gains = jnp.broadcast_to(gains, (N_Z, 8, block))

    result = pl.pallas_call(
        heads_kernel,
        grid=(N_Z,),
        in_specs=[
            pl.BlockSpec((block, rows), lambda i: (i, 0)),
            pl.BlockSpec((1, outs, block), lambda i: (i, 0, 0)),
            pl.BlockSpec((1, 8, block), lambda i: (i, 0, 0)),
            pl.BlockSpec((2, rows), lambda i: (0, 0)),
            pl.BlockSpec((2 * rank, rows), lambda i: (0, 0)),
            pl.BlockSpec((size, rank), lambda i: (0, 0)),
            pl.BlockSpec((size, 2 * images), lambda i: (0, 0)),
        ],
        out_specs=pl.BlockSpec((rows, size), lambda i: (0, 0)),
        out_shape=jax.ShapeDtypeStruct((rows, size), jnp.bfloat16),
        scratch_shapes=[pltpu.VMEM((outs, rows), jnp.float32)],
        compiler_params=pltpu.CompilerParams(
            dimension_semantics=("arbitrary",), vmem_limit_bytes=56 * 2**20
        ),
        cost_estimate=pl.CostEstimate(
            flops=2 * full * outs * rows, bytes_accessed=12 * 2**20, transcendentals=0
        ),
        name="heads",
    )(whole, weights, gains, stat, low, b_shared.reshape(size, rank), scale)
    return result.reshape(rows, 1, size)


def solution(mesh):
    return jax.shard_map(
        local,
        mesh=mesh,
        in_specs=(
            P("dp", "mp"),
            P("mp"),
            P("dp"),
            P(None, "mp", None),
            P("dp", "mp"),
            P("mp", None, None),
            P(),
            P(),
            P(None, "mp", None),
            P(None, "mp", None),
        ),
        out_specs=P("dp", "mp", None),
        check_vma=False,
    )
```

```python
import jax
import jax.numpy as jnp
from jax import lax
from jax.experimental import pallas as pl
from jax.experimental.pallas import tpu as pltpu
from jax.sharding import PartitionSpec as P

eps = 1e-06
N_Y, N_Z = 4, 8
along_y = [[y * N_Z + z for y in range(N_Y)] for z in range(N_Z)]
along_z = [[y * N_Z + z for z in range(N_Z)] for y in range(N_Y)]


def terms(values):
    high = lax.reduce_precision(values, 8, 7)
    rest = values - high
    middle = lax.reduce_precision(rest, 8, 7)
    return [part.astype(jnp.bfloat16) for part in (high, middle, rest - middle)]


def unit_columns(values):
    centre = values - jnp.mean(values, axis=0, keepdims=True)
    spread = jnp.mean(centre * centre, axis=0, keepdims=True)
    return (centre * lax.rsqrt(spread + eps)).astype(jnp.bfloat16)


def projected(x, w, gain, stat):
    gain = jnp.transpose(jnp.broadcast_to(gain, (8, x.shape[0])))[:, :1]
    normed = ((x.astype(jnp.float32) - stat[0:1]) * stat[1:2] * gain).astype(jnp.bfloat16)
    return lax.dot_general(
        w.reshape(x.shape[0], w.shape[-1]),
        normed,
        (((0,), (0,)), ((), ())),
        preferred_element_type=jnp.float32,
    )


def heads_kernel(
    x_ref, w_ref, gain_ref, stat_ref, low_ref, b_ref, scale_ref, out_ref, acc_ref
):
    step = pl.program_id(0)

    @pl.when(step == 0)
    def _():
        acc_ref[...] = jnp.zeros_like(acc_ref)

    stat = stat_ref[...]
    acc_ref[...] += sum(
        projected(x_ref[n], w_ref[:, n], gain_ref[n], stat) for n in range(x_ref.shape[0])
    )

    @pl.when(step == pl.num_programs(0) - 1)
    def _():
        size = b_ref.shape[0]
        images = scale_ref.shape[1] // 2
        patches = x_ref.shape[2] // images
        rank = b_ref.shape[1]
        up_q = jnp.dot(b_ref[...], low_ref[:rank], preferred_element_type=jnp.float32)
        up_v = jnp.dot(b_ref[...], low_ref[rank:], preferred_element_type=jnp.float32)
        for i in range(images):
            cols = slice(i * patches, (i + 1) * patches)
            query = acc_ref[:size, cols] + up_q[:, cols] * scale_ref[:, i : i + 1]
            value = (
                acc_ref[2 * size :, cols] + up_v[:, cols] * scale_ref[:, images + i : images + i + 1]
            ).astype(jnp.bfloat16)
            query = unit_columns(query)
            key = unit_columns(acc_ref[size : 2 * size, cols])
            scores = lax.dot_general(
                key, query, (((0,), (0,)), ((), ())), preferred_element_type=jnp.float32
            )
            expo = jnp.exp(scores * (1.0 / jnp.sqrt(jnp.float32(size))))
            probs = (expo / jnp.sum(expo, axis=0, keepdims=True)).astype(jnp.bfloat16)
            mixed = jnp.dot(value, probs, preferred_element_type=jnp.float32)
            out_ref[cols, :] = jnp.transpose(mixed).astype(out_ref.dtype)


def local(
    activations, ln_gain, task_ids, w_qkv, a_shared, b_shared, d_query, d_value, b_query, b_value
):
    rows, width = activations.shape
    images = task_ids.shape[0]
    patches = rows // images
    size = b_shared.shape[1]
    rank = b_shared.shape[2]
    tasks = d_query.shape[0]
    parts = lax.axis_size("mp")
    full = width * parts
    own = rank // parts
    groups = lax.axis_size("dp")

    flat = activations.T
    by_y = lax.all_gather(flat, "mp", axis=0, tiled=True, axis_index_groups=along_y)
    whole = lax.all_gather(by_y, "mp", axis=0, tiled=True, axis_index_groups=along_z)

    block = N_Y * width
    quarter = rank // N_Y
    down = lax.all_to_all(jnp.broadcast_to(a_shared, (groups, rank // groups, width)), "dp", 0, 0)
    down = jnp.concatenate(
        (
            down.reshape(N_Y, quarter, width),
            jnp.broadcast_to(ln_gain, (N_Y, 1, width)),
            jnp.zeros((N_Y, 15, width), jnp.bfloat16),
        ),
        axis=1,
    )
    down = lax.all_to_all(down, "mp", 0, 0, axis_index_groups=along_y)
    gain = down[:, quarter].reshape(block)
    down = down[:, :quarter].transpose(1, 0, 2).reshape(quarter, block)
    values = by_y.astype(jnp.float32)
    mean_here = jnp.mean(values, axis=0)
    centre = values - mean_here
    square_here = jnp.sum(centre * centre, axis=0)
    gain_here = gain.astype(jnp.float32)
    partial = jnp.dot(
        down, (centre * gain_here[:, None]).astype(jnp.bfloat16), preferred_element_type=jnp.float32
    )
    down_gain = jnp.sum(down.astype(jnp.float32) * gain_here, axis=1).reshape(N_Z, own)
    lead = rows - (block - rows)
    last = jnp.concatenate(
        (
            *terms(down_gain),
            jnp.zeros((N_Z, lead - 3 * own), jnp.bfloat16),
            jnp.broadcast_to(gain, (N_Z, block)),
        ),
        axis=1,
    )
    stats = jnp.stack(terms(mean_here) + terms(square_here), axis=0)
    sent = jnp.concatenate(
        (
            partial.astype(jnp.bfloat16).reshape(N_Z, own, rows),
            jnp.broadcast_to(stats, (N_Z, 6, rows)),
            last.reshape(N_Z, 2, rows),
        ),
        axis=1,
    )
    came = lax.all_to_all(sent, "mp", 0, 0, axis_index_groups=along_z).astype(jnp.float32)
    means = came[:, own] + came[:, own + 1] + came[:, own + 2]
    squares = came[:, own + 3] + came[:, own + 4] + came[:, own + 5]
    side = came[:, own + 6 :].reshape(N_Z, 2 * rows)
    gains = side[:, lead:]
    down_gains = side[:, :own] + side[:, own : 2 * own] + side[:, 2 * own : 3 * own]
    row_mean = jnp.mean(means, axis=0)
    offset = means - row_mean
    row_var = (jnp.sum(squares, axis=0) + block * jnp.sum(offset * offset, axis=0)) / full
    row_scale = lax.rsqrt(row_var + eps)
    ranks = jnp.sum(came[:, :own] + down_gains[:, :, None] * offset[:, None, :], axis=0) * row_scale

    onehot = (task_ids[:, None] == lax.broadcasted_iota(jnp.int32, (images, tasks), 1)).astype(
        jnp.float32
    )
    highest = lax.Precision.HIGHEST
    at = lax.axis_index("mp") * own
    dq = jnp.dot(onehot, lax.dynamic_slice_in_dim(d_query, at, own, 1), precision=highest)
    dv = jnp.dot(onehot, lax.dynamic_slice_in_dim(d_value, at, own, 1), precision=highest)
    by_image = ranks.reshape(own, images, patches)
    scaled = jnp.stack((by_image * dq.T[:, :, None], by_image * dv.T[:, :, None]), axis=0)
    scaled = scaled.reshape(2 * own, rows).astype(jnp.bfloat16)
    low = lax.all_to_all(
        jnp.broadcast_to(scaled, (N_Z, 2 * own, rows)), "mp", 0, 0, axis_index_groups=along_z
    )
    low = lax.all_to_all(
        jnp.broadcast_to(low, (N_Y, N_Z, 2 * own, rows)), "mp", 0, 0, axis_index_groups=along_y
    )
    low = low.reshape(parts, 2, own, rows).transpose(1, 0, 2, 3).reshape(2 * rank, rows)

    bq = jnp.dot(onehot, b_query.reshape(tasks, size), precision=highest)
    bv = jnp.dot(onehot, b_value.reshape(tasks, size), precision=highest)
    scale = jnp.concatenate((bq, bv), axis=0).T
    stat = jnp.stack((row_mean, row_scale), axis=0)
    outs = w_qkv.shape[2]
    weights = w_qkv.reshape(N_Y, N_Z, width, outs)
    gains = gains.reshape(N_Z, 1, block)

    result = pl.pallas_call(
        heads_kernel,
        grid=(N_Z // 2,),
        in_specs=[
            pl.BlockSpec((2, block, rows), lambda i: (i, 0, 0)),
            pl.BlockSpec((N_Y, 2, width, outs), lambda i: (0, i, 0, 0)),
            pl.BlockSpec((2, 1, block), lambda i: (i, 0, 0)),
            pl.BlockSpec((2, rows), lambda i: (0, 0)),
            pl.BlockSpec((2 * rank, rows), lambda i: (0, 0)),
            pl.BlockSpec((size, rank), lambda i: (0, 0)),
            pl.BlockSpec((size, 2 * images), lambda i: (0, 0)),
        ],
        out_specs=pl.BlockSpec((rows, size), lambda i: (0, 0)),
        out_shape=jax.ShapeDtypeStruct((rows, size), jnp.bfloat16),
        scratch_shapes=[pltpu.VMEM((outs, rows), jnp.float32)],
        compiler_params=pltpu.CompilerParams(
            dimension_semantics=("arbitrary",), vmem_limit_bytes=56 * 2**20
        ),
        cost_estimate=pl.CostEstimate(
            flops=2 * full * outs * rows, bytes_accessed=12 * 2**20, transcendentals=0
        ),
        name="heads",
    )(whole.reshape(N_Z, block, rows), weights, gains, stat, low, b_shared.reshape(size, rank), scale)
    return result.reshape(rows, 1, size)


def solution(mesh):
    return jax.shard_map(
        local,
        mesh=mesh,
        in_specs=(
            P("dp", "mp"),
            P("mp"),
            P("dp"),
            P(None, "mp", None),
            P("dp", "mp"),
            P("mp", None, None),
            P(),
            P(),
            P(None, "mp", None),
            P(None, "mp", None),
        ),
        out_specs=P("dp", "mp", None),
        check_vma=False,
    )
```

```python
import jax
import jax.numpy as jnp
from jax import lax
from jax.experimental import pallas as pl
from jax.experimental.pallas import tpu as pltpu
from jax.sharding import PartitionSpec as P

eps = 1e-06
N_Y, N_Z = 4, 8
along_y = [[y * N_Z + z for y in range(N_Y)] for z in range(N_Z)]
along_z = [[y * N_Z + z for z in range(N_Z)] for y in range(N_Y)]


def terms(values):
    high = lax.reduce_precision(values, 8, 7)
    rest = values - high
    middle = lax.reduce_precision(rest, 8, 7)
    return [part.astype(jnp.bfloat16) for part in (high, middle, rest - middle)]


def unit_columns(values):
    centre = values - jnp.mean(values, axis=0, keepdims=True)
    spread = jnp.mean(centre * centre, axis=0, keepdims=True)
    return (centre * lax.rsqrt(spread + eps)).astype(jnp.bfloat16)


def projected(x, w, gain, stat):
    gain = jnp.transpose(jnp.broadcast_to(gain, (8, x.shape[0])))[:, :1]
    normed = ((x.astype(jnp.float32) - stat[0:1]) * stat[1:2] * gain).astype(jnp.bfloat16)
    return lax.dot_general(
        w.reshape(x.shape[0], w.shape[-1]),
        normed,
        (((0,), (0,)), ((), ())),
        preferred_element_type=jnp.float32,
    )


def heads_kernel(
    x_ref, w_ref, gain_ref, stat_ref, low_ref, b_ref, scale_ref, out_ref, acc_ref
):
    step = pl.program_id(0)

    @pl.when(step == 0)
    def _():
        acc_ref[...] = jnp.zeros_like(acc_ref)

    stat = stat_ref[...]
    acc_ref[...] += sum(
        projected(x_ref[n], w_ref[:, n], gain_ref[n], stat) for n in range(x_ref.shape[0])
    )

    @pl.when(step == pl.num_programs(0) - 1)
    def _():
        size = b_ref.shape[0]
        images = scale_ref.shape[1] // 2
        patches = x_ref.shape[2] // images
        rank = b_ref.shape[1]
        up_q = jnp.dot(b_ref[...], low_ref[:rank], preferred_element_type=jnp.float32)
        up_v = jnp.dot(b_ref[...], low_ref[rank:], preferred_element_type=jnp.float32)
        for i in range(images):
            cols = slice(i * patches, (i + 1) * patches)
            query = acc_ref[:size, cols] + up_q[:, cols] * scale_ref[:, i : i + 1]
            value = (
                acc_ref[2 * size :, cols] + up_v[:, cols] * scale_ref[:, images + i : images + i + 1]
            ).astype(jnp.bfloat16)
            query = unit_columns(query)
            key = unit_columns(acc_ref[size : 2 * size, cols])
            scores = lax.dot_general(
                key, query, (((0,), (0,)), ((), ())), preferred_element_type=jnp.float32
            )
            expo = jnp.exp(scores * (1.0 / jnp.sqrt(jnp.float32(size))))
            probs = (expo / jnp.sum(expo, axis=0, keepdims=True)).astype(jnp.bfloat16)
            mixed = jnp.dot(value, probs, preferred_element_type=jnp.float32)
            out_ref[cols, :] = jnp.transpose(mixed).astype(out_ref.dtype)


def local(
    activations, ln_gain, task_ids, w_qkv, a_shared, b_shared, d_query, d_value, b_query, b_value
):
    rows, width = activations.shape
    images = task_ids.shape[0]
    patches = rows // images
    size = b_shared.shape[1]
    rank = b_shared.shape[2]
    tasks = d_query.shape[0]
    parts = lax.axis_size("mp")
    full = width * parts
    own = rank // parts
    groups = lax.axis_size("dp")

    flat = activations.T
    by_y = lax.all_gather(flat, "mp", axis=0, tiled=True, axis_index_groups=along_y)
    whole = lax.all_gather(by_y, "mp", axis=0, tiled=True, axis_index_groups=along_z)

    block = N_Y * width
    quarter = rank // N_Y
    down = lax.all_to_all(jnp.broadcast_to(a_shared, (groups, rank // groups, width)), "dp", 0, 0)
    down = jnp.concatenate(
        (
            down.reshape(N_Y, quarter, width),
            jnp.broadcast_to(ln_gain, (N_Y, 1, width)),
            jnp.zeros((N_Y, 15, width), jnp.bfloat16),
        ),
        axis=1,
    )
    down = lax.all_to_all(down, "mp", 0, 0, axis_index_groups=along_y)
    gain = down[:, quarter].reshape(block)
    down = down[:, :quarter].transpose(1, 0, 2).reshape(quarter, block)
    values = by_y.astype(jnp.float32)
    mean_here = jnp.mean(values, axis=0)
    centre = values - mean_here
    square_here = jnp.sum(centre * centre, axis=0)
    gain_here = gain.astype(jnp.float32)
    partial = jnp.dot(
        down, (centre * gain_here[:, None]).astype(jnp.bfloat16), preferred_element_type=jnp.float32
    )
    down_gain = jnp.sum(down.astype(jnp.float32) * gain_here, axis=1).reshape(N_Z, own)
    lead = rows - (block - rows)
    last = jnp.concatenate(
        (
            *terms(down_gain),
            jnp.zeros((N_Z, lead - 3 * own), jnp.bfloat16),
            jnp.broadcast_to(gain, (N_Z, block)),
        ),
        axis=1,
    )
    stats = jnp.stack(terms(mean_here) + terms(square_here), axis=0)
    sent = jnp.concatenate(
        (
            partial.astype(jnp.bfloat16).reshape(N_Z, own, rows),
            jnp.broadcast_to(stats, (N_Z, 6, rows)),
            last.reshape(N_Z, 2, rows),
        ),
        axis=1,
    )
    came = lax.all_to_all(sent, "mp", 0, 0, axis_index_groups=along_z).astype(jnp.float32)
    means = came[:, own] + came[:, own + 1] + came[:, own + 2]
    squares = came[:, own + 3] + came[:, own + 4] + came[:, own + 5]
    side = came[:, own + 6 :].reshape(N_Z, 2 * rows)
    gains = side[:, lead:]
    down_gains = side[:, :own] + side[:, own : 2 * own] + side[:, 2 * own : 3 * own]
    row_mean = jnp.mean(means, axis=0)
    offset = means - row_mean
    row_var = (jnp.sum(squares, axis=0) + block * jnp.sum(offset * offset, axis=0)) / full
    row_scale = lax.rsqrt(row_var + eps)
    ranks = jnp.sum(came[:, :own] + down_gains[:, :, None] * offset[:, None, :], axis=0) * row_scale

    onehot = (task_ids[:, None] == lax.broadcasted_iota(jnp.int32, (images, tasks), 1)).astype(
        jnp.float32
    )
    highest = lax.Precision.HIGHEST
    at = lax.axis_index("mp") * own
    dq = jnp.dot(onehot, lax.dynamic_slice_in_dim(d_query, at, own, 1), precision=highest)
    dv = jnp.dot(onehot, lax.dynamic_slice_in_dim(d_value, at, own, 1), precision=highest)
    by_image = ranks.reshape(own, images, patches)
    scaled = jnp.stack((by_image * dq.T[:, :, None], by_image * dv.T[:, :, None]), axis=0)
    scaled = scaled.reshape(2 * own, rows).astype(jnp.bfloat16)
    low = lax.all_to_all(
        jnp.broadcast_to(scaled, (N_Z, 2 * own, rows)), "mp", 0, 0, axis_index_groups=along_z
    )
    low = lax.all_to_all(
        jnp.broadcast_to(low, (N_Y, N_Z, 2 * own, rows)), "mp", 0, 0, axis_index_groups=along_y
    )
    low = low.reshape(parts, 2, own, rows).transpose(1, 0, 2, 3).reshape(2 * rank, rows)

    bq = jnp.dot(onehot, b_query.reshape(tasks, size), precision=highest)
    bv = jnp.dot(onehot, b_value.reshape(tasks, size), precision=highest)
    scale = jnp.concatenate((bq, bv), axis=0).T
    stat = jnp.stack((row_mean, row_scale), axis=0)
    outs = w_qkv.shape[2]
    weights = w_qkv.reshape(N_Y, N_Z, width, outs)
    gains = gains.reshape(N_Z, 1, block)

    result = pl.pallas_call(
        heads_kernel,
        grid=(N_Z // 4,),
        in_specs=[
            pl.BlockSpec((4, block, rows), lambda i: (i, 0, 0)),
            pl.BlockSpec((N_Y, 4, width, outs), lambda i: (0, i, 0, 0)),
            pl.BlockSpec((4, 1, block), lambda i: (i, 0, 0)),
            pl.BlockSpec((2, rows), lambda i: (0, 0)),
            pl.BlockSpec((2 * rank, rows), lambda i: (0, 0)),
            pl.BlockSpec((size, rank), lambda i: (0, 0)),
            pl.BlockSpec((size, 2 * images), lambda i: (0, 0)),
        ],
        out_specs=pl.BlockSpec((rows, size), lambda i: (0, 0)),
        out_shape=jax.ShapeDtypeStruct((rows, size), jnp.bfloat16),
        scratch_shapes=[pltpu.VMEM((outs, rows), jnp.float32)],
        compiler_params=pltpu.CompilerParams(
            dimension_semantics=("arbitrary",), vmem_limit_bytes=52 * 2**20
        ),
        cost_estimate=pl.CostEstimate(
            flops=2 * full * outs * rows, bytes_accessed=12 * 2**20, transcendentals=0
        ),
        name="heads",
    )(whole.reshape(N_Z, block, rows), weights, gains, stat, low, b_shared.reshape(size, rank), scale)
    return result.reshape(rows, 1, size)


def solution(mesh):
    return jax.shard_map(
        local,
        mesh=mesh,
        in_specs=(
            P("dp", "mp"),
            P("mp"),
            P("dp"),
            P(None, "mp", None),
            P("dp", "mp"),
            P("mp", None, None),
            P(),
            P(),
            P(None, "mp", None),
            P(None, "mp", None),
        ),
        out_specs=P("dp", "mp", None),
        check_vma=False,
    )
```

```python
import jax
import jax.numpy as jnp
from jax import lax
from jax.experimental import pallas as pl
from jax.experimental.pallas import tpu as pltpu
from jax.sharding import PartitionSpec as P

eps = 1e-06
N_Y, N_Z = 4, 8
PATCHES = 256
along_y = [[y * N_Z + z for y in range(N_Y)] for z in range(N_Z)]
along_z = [[y * N_Z + z for z in range(N_Z)] for y in range(N_Y)]


def terms(values):
    high = lax.reduce_precision(values, 8, 7)
    rest = values - high
    middle = lax.reduce_precision(rest, 8, 7)
    return [part.astype(jnp.bfloat16) for part in (high, middle, rest - middle)]


def unit_columns(values):
    centre = values - jnp.mean(values, axis=0, keepdims=True)
    spread = jnp.mean(centre * centre, axis=0, keepdims=True)
    return (centre * lax.rsqrt(spread + eps)).astype(jnp.bfloat16)


def projected(x, w, gain, stat):
    gain = jnp.transpose(jnp.broadcast_to(gain, (8, x.shape[0])))[:, :1]
    normed = ((x.astype(jnp.float32) - stat[0:1]) * stat[1:2] * gain).astype(jnp.bfloat16)
    return lax.dot_general(
        w.reshape(x.shape[0], w.shape[-1]),
        normed,
        (((0,), (0,)), ((), ())),
        preferred_element_type=jnp.float32,
    )


def heads_kernel(
    x_ref, w_ref, gain_ref, stat_ref, lift_ref, out_ref, acc_ref
):
    step = pl.program_id(0)

    @pl.when(step == 0)
    def _():
        acc_ref[...] = jnp.zeros_like(acc_ref)

    stat = stat_ref[...]
    acc_ref[...] += sum(
        projected(x_ref[n], w_ref[:, n], gain_ref[n], stat) for n in range(x_ref.shape[0])
    )

    @pl.when(step == pl.num_programs(0) - 1)
    def _():
        size = out_ref.shape[1]
        patches = PATCHES
        for i in range(out_ref.shape[0] // patches):
            cols = slice(i * patches, (i + 1) * patches)
            query = acc_ref[:size, cols] + lift_ref[:size, cols]
            value = (acc_ref[2 * size :, cols] + lift_ref[size:, cols]).astype(jnp.bfloat16)
            query = unit_columns(query)
            key = unit_columns(acc_ref[size : 2 * size, cols])
            scores = lax.dot_general(
                key, query, (((0,), (0,)), ((), ())), preferred_element_type=jnp.float32
            )
            expo = jnp.exp(scores * (1.0 / jnp.sqrt(jnp.float32(size))))
            probs = (expo / jnp.sum(expo, axis=0, keepdims=True)).astype(jnp.bfloat16)
            mixed = jnp.dot(value, probs, preferred_element_type=jnp.float32)
            out_ref[cols, :] = jnp.transpose(mixed).astype(out_ref.dtype)


def local(
    activations, ln_gain, task_ids, w_qkv, a_shared, b_shared, d_query, d_value, b_query, b_value
):
    rows, width = activations.shape
    images = task_ids.shape[0]
    patches = rows // images
    size = b_shared.shape[1]
    rank = b_shared.shape[2]
    tasks = d_query.shape[0]
    parts = lax.axis_size("mp")
    full = width * parts
    own = rank // parts
    groups = lax.axis_size("dp")

    flat = activations.T
    by_y = lax.all_gather(flat, "mp", axis=0, tiled=True, axis_index_groups=along_y)
    whole = lax.all_gather(by_y, "mp", axis=0, tiled=True, axis_index_groups=along_z)

    block = N_Y * width
    quarter = rank // N_Y
    down = lax.all_to_all(jnp.broadcast_to(a_shared, (groups, rank // groups, width)), "dp", 0, 0)
    down = jnp.concatenate(
        (
            down.reshape(N_Y, quarter, width),
            jnp.broadcast_to(ln_gain, (N_Y, 1, width)),
            jnp.zeros((N_Y, 15, width), jnp.bfloat16),
        ),
        axis=1,
    )
    down = lax.all_to_all(down, "mp", 0, 0, axis_index_groups=along_y)
    gain = down[:, quarter].reshape(block)
    down = down[:, :quarter].transpose(1, 0, 2).reshape(quarter, block)
    values = by_y.astype(jnp.float32)
    mean_here = jnp.mean(values, axis=0)
    centre = values - mean_here
    square_here = jnp.sum(centre * centre, axis=0)
    gain_here = gain.astype(jnp.float32)
    partial = jnp.dot(
        down, (centre * gain_here[:, None]).astype(jnp.bfloat16), preferred_element_type=jnp.float32
    )
    down_gain = jnp.sum(down.astype(jnp.float32) * gain_here, axis=1).reshape(N_Z, own)
    lead = rows - (block - rows)
    last = jnp.concatenate(
        (
            *terms(down_gain),
            jnp.zeros((N_Z, lead - 3 * own), jnp.bfloat16),
            jnp.broadcast_to(gain, (N_Z, block)),
        ),
        axis=1,
    )
    stats = jnp.stack(terms(mean_here) + terms(square_here), axis=0)
    sent = jnp.concatenate(
        (
            partial.astype(jnp.bfloat16).reshape(N_Z, own, rows),
            jnp.broadcast_to(stats, (N_Z, 6, rows)),
            last.reshape(N_Z, 2, rows),
        ),
        axis=1,
    )
    came = lax.all_to_all(sent, "mp", 0, 0, axis_index_groups=along_z).astype(jnp.float32)
    means = came[:, own] + came[:, own + 1] + came[:, own + 2]
    squares = came[:, own + 3] + came[:, own + 4] + came[:, own + 5]
    side = came[:, own + 6 :].reshape(N_Z, 2 * rows)
    gains = side[:, lead:]
    down_gains = side[:, :own] + side[:, own : 2 * own] + side[:, 2 * own : 3 * own]
    row_mean = jnp.mean(means, axis=0)
    offset = means - row_mean
    row_var = (jnp.sum(squares, axis=0) + block * jnp.sum(offset * offset, axis=0)) / full
    row_scale = lax.rsqrt(row_var + eps)
    ranks = jnp.sum(came[:, :own] + down_gains[:, :, None] * offset[:, None, :], axis=0) * row_scale

    onehot = (task_ids[:, None] == lax.broadcasted_iota(jnp.int32, (images, tasks), 1)).astype(
        jnp.float32
    )
    highest = lax.Precision.HIGHEST
    at = lax.axis_index("mp") * own
    dq = jnp.dot(onehot, lax.dynamic_slice_in_dim(d_query, at, own, 1), precision=highest)
    dv = jnp.dot(onehot, lax.dynamic_slice_in_dim(d_value, at, own, 1), precision=highest)
    by_image = ranks.reshape(own, images, patches)
    scaled = jnp.stack((by_image * dq.T[:, :, None], by_image * dv.T[:, :, None]), axis=0)
    scaled = scaled.reshape(2 * own, rows).astype(jnp.bfloat16)
    low = lax.all_to_all(
        jnp.broadcast_to(scaled, (N_Z, 2 * own, rows)), "mp", 0, 0, axis_index_groups=along_z
    )
    low = lax.all_to_all(
        jnp.broadcast_to(low, (N_Y, N_Z, 2 * own, rows)), "mp", 0, 0, axis_index_groups=along_y
    )
    low = low.reshape(parts, 2, own, rows).transpose(1, 0, 2, 3).reshape(2 * rank, rows)

    bq = jnp.dot(onehot, b_query.reshape(tasks, size), precision=highest)
    bv = jnp.dot(onehot, b_value.reshape(tasks, size), precision=highest)
    up = b_shared.reshape(size, rank)
    lift = jnp.concatenate(
        (
            jnp.dot(up, low[:rank], preferred_element_type=jnp.float32)
            * jnp.repeat(bq.T, patches, axis=1),
            jnp.dot(up, low[rank:], preferred_element_type=jnp.float32)
            * jnp.repeat(bv.T, patches, axis=1),
        ),
        axis=0,
    )
    stat = jnp.stack((row_mean, row_scale), axis=0)
    outs = w_qkv.shape[2]
    weights = w_qkv.reshape(N_Y, N_Z, width, outs)
    gains = gains.reshape(N_Z, 1, block)

    result = pl.pallas_call(
        heads_kernel,
        grid=(N_Z // 4,),
        in_specs=[
            pl.BlockSpec((4, block, rows), lambda i: (i, 0, 0)),
            pl.BlockSpec((N_Y, 4, width, outs), lambda i: (0, i, 0, 0)),
            pl.BlockSpec((4, 1, block), lambda i: (i, 0, 0)),
            pl.BlockSpec((2, rows), lambda i: (0, 0)),
            pl.BlockSpec((2 * size, rows), lambda i: (0, 0)),
        ],
        out_specs=pl.BlockSpec((rows, size), lambda i: (0, 0)),
        out_shape=jax.ShapeDtypeStruct((rows, size), jnp.bfloat16),
        scratch_shapes=[pltpu.VMEM((outs, rows), jnp.float32)],
        compiler_params=pltpu.CompilerParams(
            dimension_semantics=("arbitrary",), vmem_limit_bytes=52 * 2**20
        ),
        cost_estimate=pl.CostEstimate(
            flops=2 * full * outs * rows, bytes_accessed=12 * 2**20, transcendentals=0
        ),
        name="heads",
    )(whole.reshape(N_Z, block, rows), weights, gains, stat, lift)
    return result.reshape(rows, 1, size)


def solution(mesh):
    return jax.shard_map(
        local,
        mesh=mesh,
        in_specs=(
            P("dp", "mp"),
            P("mp"),
            P("dp"),
            P(None, "mp", None),
            P("dp", "mp"),
            P("mp", None, None),
            P(),
            P(),
            P(None, "mp", None),
            P(None, "mp", None),
        ),
        out_specs=P("dp", "mp", None),
        check_vma=False,
    )
```

```python
import jax
import jax.numpy as jnp
from jax import lax
from jax.experimental import pallas as pl
from jax.experimental.pallas import tpu as pltpu
from jax.sharding import PartitionSpec as P

eps = 1e-06
N_Y, N_Z = 4, 8
along_y = [[y * N_Z + z for y in range(N_Y)] for z in range(N_Z)]
along_z = [[y * N_Z + z for z in range(N_Z)] for y in range(N_Y)]


def terms(values):
    high = lax.reduce_precision(values, 8, 7)
    rest = values - high
    middle = lax.reduce_precision(rest, 8, 7)
    return [part.astype(jnp.bfloat16) for part in (high, middle, rest - middle)]


def unit_columns(values):
    centre = values - jnp.mean(values, axis=0, keepdims=True)
    spread = jnp.mean(centre * centre, axis=0, keepdims=True)
    return (centre * lax.rsqrt(spread + eps)).astype(jnp.bfloat16)


def projected(x, w, gain, stat):
    gain = jnp.transpose(jnp.broadcast_to(gain, (8, x.shape[0])))[:, :1]
    normed = ((x.astype(jnp.float32) - stat[0:1]) * stat[1:2] * gain).astype(jnp.bfloat16)
    return lax.dot_general(
        w.reshape(x.shape[0], w.shape[-1]),
        normed,
        (((0,), (0,)), ((), ())),
        preferred_element_type=jnp.float32,
    )


def heads_kernel(
    x_ref, w_ref, gain_ref, stat_ref, low_ref, b_ref, scale_ref, out_ref, acc_ref
):
    step = pl.program_id(0)

    stat = stat_ref[...]
    new = sum(projected(x_ref[n], w_ref[:, n], gain_ref[n], stat) for n in range(x_ref.shape[0]))

    @pl.when(step == 0)
    def _():
        acc_ref[...] = new

    @pl.when(step > 0)
    def _():
        acc_ref[...] += new

    @pl.when(step == pl.num_programs(0) - 1)
    def _():
        size = b_ref.shape[0]
        images = scale_ref.shape[1] // 2
        patches = x_ref.shape[2] // images
        rank = b_ref.shape[1]
        up_q = jnp.dot(b_ref[...], low_ref[:rank], preferred_element_type=jnp.float32)
        up_v = jnp.dot(b_ref[...], low_ref[rank:], preferred_element_type=jnp.float32)
        for i in range(images):
            cols = slice(i * patches, (i + 1) * patches)
            query = acc_ref[:size, cols] + up_q[:, cols] * scale_ref[:, i : i + 1]
            value = (
                acc_ref[2 * size :, cols] + up_v[:, cols] * scale_ref[:, images + i : images + i + 1]
            ).astype(jnp.bfloat16)
            query = unit_columns(query)
            key = unit_columns(acc_ref[size : 2 * size, cols])
            scores = lax.dot_general(
                key, query, (((0,), (0,)), ((), ())), preferred_element_type=jnp.float32
            )
            expo = jnp.exp(scores * (1.0 / jnp.sqrt(jnp.float32(size))))
            probs = (expo / jnp.sum(expo, axis=0, keepdims=True)).astype(jnp.bfloat16)
            mixed = jnp.dot(value, probs, preferred_element_type=jnp.float32)
            out_ref[cols, :] = jnp.transpose(mixed).astype(out_ref.dtype)


def local(
    activations, ln_gain, task_ids, w_qkv, a_shared, b_shared, d_query, d_value, b_query, b_value
):
    rows, width = activations.shape
    images = task_ids.shape[0]
    patches = rows // images
    size = b_shared.shape[1]
    rank = b_shared.shape[2]
    tasks = d_query.shape[0]
    parts = lax.axis_size("mp")
    full = width * parts
    own = rank // parts
    groups = lax.axis_size("dp")

    flat = activations.T
    by_y = lax.all_gather(flat, "mp", axis=0, tiled=True, axis_index_groups=along_y)
    whole = lax.all_gather(by_y, "mp", axis=0, tiled=True, axis_index_groups=along_z)

    block = N_Y * width
    quarter = rank // N_Y
    down = lax.all_to_all(jnp.broadcast_to(a_shared, (groups, rank // groups, width)), "dp", 0, 0)
    down = jnp.concatenate(
        (
            down.reshape(N_Y, quarter, width),
            jnp.broadcast_to(ln_gain, (N_Y, 1, width)),
            jnp.zeros((N_Y, 15, width), jnp.bfloat16),
        ),
        axis=1,
    )
    down = lax.all_to_all(down, "mp", 0, 0, axis_index_groups=along_y)
    gain = down[:, quarter].reshape(block)
    down = down[:, :quarter].transpose(1, 0, 2).reshape(quarter, block)
    values = by_y.astype(jnp.float32)
    mean_here = jnp.mean(values, axis=0)
    centre = values - mean_here
    square_here = jnp.sum(centre * centre, axis=0)
    gain_here = gain.astype(jnp.float32)
    partial = jnp.dot(
        down, (centre * gain_here[:, None]).astype(jnp.bfloat16), preferred_element_type=jnp.float32
    )
    down_gain = jnp.sum(down.astype(jnp.float32) * gain_here, axis=1).reshape(N_Z, own)
    lead = rows - (block - rows)
    last = jnp.concatenate(
        (
            *terms(down_gain),
            jnp.zeros((N_Z, lead - 3 * own), jnp.bfloat16),
            jnp.broadcast_to(gain, (N_Z, block)),
        ),
        axis=1,
    )
    stats = jnp.stack(terms(mean_here) + terms(square_here), axis=0)
    sent = jnp.concatenate(
        (
            partial.astype(jnp.bfloat16).reshape(N_Z, own, rows),
            jnp.broadcast_to(stats, (N_Z, 6, rows)),
            last.reshape(N_Z, 2, rows),
        ),
        axis=1,
    )
    came = lax.all_to_all(sent, "mp", 0, 0, axis_index_groups=along_z).astype(jnp.float32)
    means = came[:, own] + came[:, own + 1] + came[:, own + 2]
    squares = came[:, own + 3] + came[:, own + 4] + came[:, own + 5]
    side = came[:, own + 6 :].reshape(N_Z, 2 * rows)
    gains = side[:, lead:]
    down_gains = side[:, :own] + side[:, own : 2 * own] + side[:, 2 * own : 3 * own]
    row_mean = jnp.mean(means, axis=0)
    offset = means - row_mean
    row_var = (jnp.sum(squares, axis=0) + block * jnp.sum(offset * offset, axis=0)) / full
    row_scale = lax.rsqrt(row_var + eps)
    ranks = jnp.sum(came[:, :own] + down_gains[:, :, None] * offset[:, None, :], axis=0) * row_scale

    onehot = (task_ids[:, None] == lax.broadcasted_iota(jnp.int32, (images, tasks), 1)).astype(
        jnp.float32
    )
    highest = lax.Precision.HIGHEST
    at = lax.axis_index("mp") * own
    dq = jnp.dot(onehot, lax.dynamic_slice_in_dim(d_query, at, own, 1), precision=highest)
    dv = jnp.dot(onehot, lax.dynamic_slice_in_dim(d_value, at, own, 1), precision=highest)
    by_image = ranks.reshape(own, images, patches)
    scaled = jnp.stack((by_image * dq.T[:, :, None], by_image * dv.T[:, :, None]), axis=0)
    scaled = scaled.reshape(2 * own, rows).astype(jnp.bfloat16)
    low = lax.all_to_all(
        jnp.broadcast_to(scaled, (N_Z, 2 * own, rows)), "mp", 0, 0, axis_index_groups=along_z
    )
    low = lax.all_to_all(
        jnp.broadcast_to(low, (N_Y, N_Z, 2 * own, rows)), "mp", 0, 0, axis_index_groups=along_y
    )
    low = low.reshape(parts, 2, own, rows).transpose(1, 0, 2, 3).reshape(2 * rank, rows)

    bq = jnp.dot(onehot, b_query.reshape(tasks, size), precision=highest)
    bv = jnp.dot(onehot, b_value.reshape(tasks, size), precision=highest)
    scale = jnp.concatenate((bq, bv), axis=0).T
    stat = jnp.stack((row_mean, row_scale), axis=0)
    outs = w_qkv.shape[2]
    weights = w_qkv.reshape(N_Y, N_Z, width, outs)
    gains = gains.reshape(N_Z, 1, block)

    result = pl.pallas_call(
        heads_kernel,
        grid=(N_Z // 4,),
        in_specs=[
            pl.BlockSpec((4, block, rows), lambda i: (i, 0, 0)),
            pl.BlockSpec((N_Y, 4, width, outs), lambda i: (0, i, 0, 0)),
            pl.BlockSpec((4, 1, block), lambda i: (i, 0, 0)),
            pl.BlockSpec((2, rows), lambda i: (0, 0)),
            pl.BlockSpec((2 * rank, rows), lambda i: (0, 0)),
            pl.BlockSpec((size, rank), lambda i: (0, 0)),
            pl.BlockSpec((size, 2 * images), lambda i: (0, 0)),
        ],
        out_specs=pl.BlockSpec((rows, size), lambda i: (0, 0)),
        out_shape=jax.ShapeDtypeStruct((rows, size), jnp.bfloat16),
        scratch_shapes=[pltpu.VMEM((outs, rows), jnp.float32)],
        compiler_params=pltpu.CompilerParams(
            dimension_semantics=("arbitrary",), vmem_limit_bytes=52 * 2**20
        ),
        cost_estimate=pl.CostEstimate(
            flops=2 * full * outs * rows, bytes_accessed=12 * 2**20, transcendentals=0
        ),
        name="heads",
    )(whole.reshape(N_Z, block, rows), weights, gains, stat, low, b_shared.reshape(size, rank), scale)
    return result.reshape(rows, 1, size)


def solution(mesh):
    return jax.shard_map(
        local,
        mesh=mesh,
        in_specs=(
            P("dp", "mp"),
            P("mp"),
            P("dp"),
            P(None, "mp", None),
            P("dp", "mp"),
            P("mp", None, None),
            P(),
            P(),
            P(None, "mp", None),
            P(None, "mp", None),
        ),
        out_specs=P("dp", "mp", None),
        check_vma=False,
    )
```
